32 devices in a mesh: dp: 4 (over y, x), tensor: 8 (over z, core).
Axes of the slice: x: 2, y: 2, z: 4, core: 2. Of those that a mesh axis runs over, the one named last changes fastest.
Arguments:
- tokens_in: bfloat16 [4096, 8192], P('dp', 'tensor'), may hold values from -6 to 6
- out_grad: bfloat16 [4096, 8192], P('dp', 'tensor'), may hold values from -6 to 6
- left_up: bfloat16 [8192, 1024], P('tensor'), may hold values from -0.1875 to 0.1875
- right_up: bfloat16 [8192, 4096], P('tensor'), may hold values from -0.1875 to 0.1875
- left_down: bfloat16 [32768, 1024], P('tensor'), may hold values from -0.09375 to 0.09375
- right_down: bfloat16 [8192, 1024], P('tensor'), may hold values from -0.1875 to 0.1875
Outputs:
- layer_out: bfloat16 [4096, 8192], P('dp', 'tensor')
- input_grad: bfloat16 [4096, 8192], P('dp', 'tensor')
- grad_left_up: bfloat16 [8192, 1024], P('tensor')
- grad_right_up: bfloat16 [8192, 4096], P('tensor')
- grad_left_down: bfloat16 [32768, 1024], P('tensor')
- grad_right_down: bfloat16 [8192, 1024], P('tensor')
The draws below stay inside these ranges and needn't reach their ends.
All inputs are finite; a program needn't handle non-finite values.
Results may differ from the reference program's by a relative error of at most 0.0075.
Values may be sent and summed in bfloat16 or wider, within the bound.
A program may use at most 192 MiB of HBM per device.

```python
import jax
import jax.numpy as jnp

D = 8192
FF = 32768
BLOCKS = 8
BLK = 1024
FBLK = 4096
TOKENS = 4096


def steps_of(key, extent, pieces, smallest, largest):
    level, own = 1.0, jax.random.fold_in(key, 6)
    for dim, parts in pieces:
        draws = jnp.exp(jax.random.uniform(jax.random.fold_in(own, dim), (parts,), jnp.float32, smallest / len(pieces), largest / len(pieces)))
        level = level * jnp.repeat(draws, extent[dim] // parts).reshape([-1 if axis == dim else 1 for axis in range(len(extent))])
    return level


def normal_values(own_key, shape, width, bound, split=(), kind=jnp.bfloat16):
    values = jax.random.normal(own_key, shape, jnp.float32) * width
    if len(split) > 0:
        values = steps_of(own_key, shape, split, -0.22, 0.18) * values
    return jnp.clip(values, min=-bound, max=bound).astype(kind)


def setup_inputs(seed: int = 0) -> dict:
    splits = jax.random.split(jax.random.key(seed), 7)
    tokens_in = normal_values(splits[0], (TOKENS, D), 1.0, 6.0, ((0, 4), (1, 8)))
    out_grad = normal_values(splits[1], (TOKENS, D), 1.0, 6.0, ((0, 4), (1, 8)))
    left_up = normal_values(splits[2], (D, BLK), BLK ** -0.5, 0.1875, ((0, 8),))
    right_up = normal_values(splits[3], (D, FBLK), BLK ** -0.5, 0.1875, ((0, 8),))
    left_down = normal_values(splits[4], (FF, BLK), FBLK ** -0.5, 0.09375, ((0, 8),))
    right_down = normal_values(splits[5], (D, BLK), BLK ** -0.5, 0.1875, ((0, 8),))
    return dict(tokens_in=tokens_in, out_grad=out_grad, left_up=left_up, right_up=right_up, left_down=left_down, right_down=right_down)


def permute(values):
    count = values.shape[0]
    sub = BLK // BLOCKS
    return values.reshape(count, BLOCKS, BLOCKS, sub).transpose(0, 2, 1, 3).reshape(count, -1)

def blockdot(values, weights, width_in, width_out):
    count = values.shape[0]
    left = values.reshape(count, BLOCKS, width_in).astype(jnp.float32)
    right = weights.reshape(BLOCKS, width_in, width_out).astype(jnp.float32)
    return jnp.einsum('nbk,bkc->nbc', left, right).reshape(count, BLOCKS * width_out)

def blockdot_t(grads, weights, width_in, width_out):
    count = grads.shape[0]
    left = grads.reshape(count, BLOCKS, width_out).astype(jnp.float32)
    right = weights.reshape(BLOCKS, width_in, width_out).astype(jnp.float32)
    return jnp.einsum('nbc,bkc->nbk', left, right).reshape(count, BLOCKS * width_in)

def outer_sum(values, grads, width_in, width_out):
    count = values.shape[0]
    left = values.reshape(count, BLOCKS, width_in).astype(jnp.float32)
    right = grads.reshape(count, BLOCKS, width_out).astype(jnp.float32)
    return jnp.einsum('nbk,nbc->bkc', left, right).reshape(BLOCKS * width_in, width_out)

def gelu_tanh(values):
    return jax.nn.gelu(values, approximate=True)

def reference(tokens_in, out_grad, left_up, right_up, left_down, right_down):
    first = blockdot(tokens_in, left_up, BLK, BLK).astype(jnp.bfloat16)
    mixed_up = permute(first)
    pre = blockdot(mixed_up, right_up, BLK, FBLK)
    hidden = gelu_tanh(pre).astype(jnp.bfloat16)
    third = blockdot(hidden, left_down, FBLK, BLK).astype(jnp.bfloat16)
    mixed_down = permute(third)
    layer_out = blockdot(mixed_down, right_down, BLK, BLK).astype(jnp.bfloat16)
    grad_right_down = outer_sum(mixed_down, out_grad, BLK, BLK).astype(jnp.bfloat16)
    back_mixed_down = blockdot_t(out_grad, right_down, BLK, BLK).astype(jnp.bfloat16)
    back_third = permute(back_mixed_down)
    grad_left_down = outer_sum(hidden, back_third, FBLK, BLK).astype(jnp.bfloat16)
    back_hidden = blockdot_t(back_third, left_down, FBLK, BLK)
    back_pre = jax.vjp(gelu_tanh, pre)[1](back_hidden)[0].astype(jnp.bfloat16)
    grad_right_up = outer_sum(mixed_up, back_pre, BLK, FBLK).astype(jnp.bfloat16)
    back_mixed_up = blockdot_t(back_pre, right_up, BLK, FBLK).astype(jnp.bfloat16)
    back_first = permute(back_mixed_up)
    grad_left_up = outer_sum(tokens_in, back_first, BLK, BLK).astype(jnp.bfloat16)
    input_grad = blockdot_t(back_first, left_up, BLK, BLK).astype(jnp.bfloat16)
    return (layer_out, input_grad, grad_left_up, grad_right_up, grad_left_down, grad_right_down)
```

```python
import jax
import jax.numpy as jnp
from jax import lax
from jax.sharding import PartitionSpec as P

F32 = jnp.float32
BF16 = jnp.bfloat16


def gelu_tanh(values):
    return jax.nn.gelu(values, approximate=True)


def dot(left, right, left_dim, right_dim):
    return lax.dot_general(
        left, right, (((left_dim,), (right_dim,)), ((), ())), preferred_element_type=F32
    )


def swap_blocks(values, blocks):
    tok_rows, width = values.shape
    sub = width // blocks
    parts = values.reshape(tok_rows, blocks, sub).transpose(1, 0, 2)
    parts = lax.all_to_all(parts, "tensor", split_axis=0, concat_axis=0, tiled=True)
    return parts.transpose(1, 0, 2).reshape(tok_rows, width)


def exchange(values, bit):
    size = lax.axis_size("dp")
    return lax.ppermute(values, "dp", [(i, i ^ (1 << bit)) for i in range(size)])


def start_sum(left, right, bits):
    me = lax.axis_index("dp")
    half = left.shape[1] // 2
    mine = (me >> bits[0]) & 1
    away = dot(lax.dynamic_slice_in_dim(left, (1 - mine) * half, half, 1), right, 0, 0).astype(BF16)
    got = exchange(away, bits[0])
    kept = dot(lax.dynamic_slice_in_dim(left, mine * half, half, 1), right, 0, 0)
    return kept + got.astype(F32)


def finish_sum(total, bits):
    me = lax.axis_index("dp")
    for bit in bits[1:]:
        half = total.shape[0] // 2
        mine = (me >> bit) & 1
        away = lax.dynamic_slice_in_dim(total, (1 - mine) * half, half, 0).astype(BF16)
        got = exchange(away, bit)
        total = lax.dynamic_slice_in_dim(total, mine * half, half, 0) + got.astype(F32)
    total = total.astype(BF16)
    for bit in reversed(bits):
        mine = (me >> bit) & 1
        got = exchange(total, bit)
        first = jnp.where(mine == 0, total, got)
        second = jnp.where(mine == 0, got, total)
        total = jnp.concatenate([first, second], axis=0)
    return total


def summed_product(left, right, pieces):
    size = lax.axis_size("dp")
    bits = list(range(size.bit_length() - 1))
    rows = left.shape[1] // pieces
    out = []
    for piece in range(pieces):
        order = bits if piece % 2 == 0 else bits[::-1]
        cut = lax.slice_in_dim(left, piece * rows, (piece + 1) * rows, axis=1)
        if order:
            out.append(finish_sum(start_sum(cut, right, order), order))
        else:
            out.append(dot(cut, right, 0, 0).astype(BF16))
    return jnp.concatenate(out, axis=0)


def on_device(tokens_in, out_grad, left_up, right_up, left_down, right_down):
    blocks = lax.axis_size("tensor")
    first = dot(tokens_in, left_up, 1, 0).astype(BF16)
    mixed_up = swap_blocks(first, blocks)
    back_mixed_down = dot(out_grad, right_down, 1, 1).astype(BF16)
    back_third = swap_blocks(back_mixed_down, blocks)

    pre_act = dot(mixed_up, right_up, 1, 0)
    hidden = gelu_tanh(pre_act).astype(BF16)
    grad_left_down = summed_product(hidden, back_third, 4)
    back_hidden = dot(back_third, left_down, 1, 1)
    back_pre = jax.vjp(gelu_tanh, pre_act)[1](back_hidden)[0].astype(BF16)
    grad_right_up = summed_product(mixed_up, back_pre, 4)
    third = dot(hidden, left_down, 1, 0).astype(BF16)
    mixed_down = swap_blocks(third, blocks)
    back_mixed_up = dot(back_pre, right_up, 1, 1).astype(BF16)
    back_first = swap_blocks(back_mixed_up, blocks)

    grad_right_down = summed_product(mixed_down, out_grad, 2)
    layer_out = dot(mixed_down, right_down, 1, 0).astype(BF16)
    grad_left_up = summed_product(tokens_in, back_first, 2)
    input_grad = dot(back_first, left_up, 1, 1).astype(BF16)
    return layer_out, input_grad, grad_left_up, grad_right_up, grad_left_down, grad_right_down


def solution(mesh):
    specs = (P("dp", "tensor"),) * 2 + (P("tensor", None),) * 4
    return jax.shard_map(on_device, mesh=mesh, in_specs=specs, out_specs=specs, check_vma=False)
```

```python
import jax
import jax.numpy as jnp
from jax import lax
from jax.experimental import pallas as pl
from jax.sharding import PartitionSpec as P

F32 = jnp.float32
BF16 = jnp.bfloat16


def gelu_tanh(values):
    return jax.nn.gelu(values, approximate=True)


def dot(left, right, left_dim, right_dim):
    return lax.dot_general(
        left, right, (((left_dim,), (right_dim,)), ((), ())), preferred_element_type=F32
    )


def nothing(*refs):
    pass


def after(values, *earlier):
    anywhere = pl.BlockSpec(memory_space=pl.ANY)
    return pl.pallas_call(
        nothing,
        out_shape=jax.ShapeDtypeStruct(values.shape, values.dtype),
        in_specs=[anywhere] * (1 + len(earlier)),
        out_specs=anywhere,
        input_output_aliases={0: 0},
    )(values, *earlier)


def swap_blocks(values, blocks):
    tok_rows, width = values.shape
    sub = width // blocks
    parts = values.reshape(tok_rows, blocks, sub).transpose(1, 0, 2)
    parts = lax.all_to_all(parts, "tensor", split_axis=0, concat_axis=0, tiled=True)
    return parts.transpose(1, 0, 2).reshape(tok_rows, width)


def exchange(values, bit):
    size = lax.axis_size("dp")
    return lax.ppermute(values, "dp", [(i, i ^ (1 << bit)) for i in range(size)])


def start_sum(left, right, bits):
    me = lax.axis_index("dp")
    half = left.shape[1] // 2
    mine = (me >> bits[0]) & 1
    away = dot(lax.dynamic_slice_in_dim(left, (1 - mine) * half, half, 1), right, 0, 0).astype(BF16)
    got = exchange(away, bits[0])
    kept = dot(lax.dynamic_slice_in_dim(left, mine * half, half, 1), right, 0, 0)
    return kept + got.astype(F32)


def scatter_sum(total, bits):
    me = lax.axis_index("dp")
    for bit in bits[1:]:
        half = total.shape[0] // 2
        mine = (me >> bit) & 1
        away = lax.dynamic_slice_in_dim(total, (1 - mine) * half, half, 0).astype(BF16)
        got = exchange(away, bit)
        total = lax.dynamic_slice_in_dim(total, mine * half, half, 0) + got.astype(F32)
    return total.astype(BF16)


def gather_sum(total, bits):
    me = lax.axis_index("dp")
    for bit in reversed(bits):
        mine = (me >> bit) & 1
        got = exchange(total, bit)
        first = jnp.where(mine == 0, total, got)
        second = jnp.where(mine == 0, got, total)
        total = jnp.concatenate([first, second], axis=0)
    return total


def piece_orders(pieces):
    bits = list(range(lax.axis_size("dp").bit_length() - 1))
    return [bits if piece % 2 == 0 else bits[::-1] for piece in range(pieces)]


def reduced_product(left, right, pieces):
    rows = left.shape[1] // pieces
    out = []
    for piece, order in enumerate(piece_orders(pieces)):
        cut = lax.slice_in_dim(left, piece * rows, (piece + 1) * rows, axis=1)
        if order:
            out.append(scatter_sum(start_sum(cut, right, order), order))
        else:
            out.append(dot(cut, right, 0, 0).astype(BF16))
    return out


def gathered(shares):
    orders = piece_orders(len(shares))
    return jnp.concatenate([gather_sum(share, order) for share, order in zip(shares, orders)], axis=0)


def on_device(tokens_in, out_grad, left_up, right_up, left_down, right_down):
    blocks = lax.axis_size("tensor")
    first = dot(tokens_in, left_up, 1, 0).astype(BF16)
    mixed_up = swap_blocks(first, blocks)
    back_mixed_down = dot(out_grad, right_down, 1, 1).astype(BF16)
    back_third = swap_blocks(back_mixed_down, blocks)

    pre_act = dot(mixed_up, right_up, 1, 0)
    hidden = gelu_tanh(pre_act).astype(BF16)
    third = dot(hidden, left_down, 1, 0).astype(BF16)
    back_third = after(back_third, third)
    mixed_down = swap_blocks(third, blocks)

    share_left_down = reduced_product(hidden, back_third, 4)
    back_hidden = dot(back_third, left_down, 1, 1)
    back_pre = jax.vjp(gelu_tanh, pre_act)[1](back_hidden)[0].astype(BF16)
    back_pre = after(back_pre, mixed_down)
    back_mixed_up = dot(back_pre, right_up, 1, 1).astype(BF16)
    back_first = swap_blocks(back_mixed_up, blocks)
    share_right_up = reduced_product(mixed_up, back_pre, 4)
    share_right_down = reduced_product(mixed_down, out_grad, 2)
    share_left_up = reduced_product(tokens_in, back_first, 2)
    share_left_down = [after(share, back_first) for share in share_left_down]

    layer_out = dot(mixed_down, right_down, 1, 0).astype(BF16)
    input_grad = dot(back_first, left_up, 1, 1).astype(BF16)
    return (
        layer_out,
        input_grad,
        gathered(share_left_up),
        gathered(share_right_up),
        gathered(share_left_down),
        gathered(share_right_down),
    )


def solution(mesh):
    specs = (P("dp", "tensor"),) * 2 + (P("tensor", None),) * 4
    return jax.shard_map(on_device, mesh=mesh, in_specs=specs, out_specs=specs, check_vma=False)
```

```python
import jax
import jax.numpy as jnp
from jax import lax
from jax.experimental import pallas as pl
from jax.sharding import PartitionSpec as P

F32 = jnp.float32
BF16 = jnp.bfloat16


def gelu_tanh(values):
    return jax.nn.gelu(values, approximate=True)


def dot(left, right, left_dim, right_dim):
    return lax.dot_general(
        left, right, (((left_dim,), (right_dim,)), ((), ())), preferred_element_type=F32
    )


def nothing(*refs):
    pass


def after(values, *earlier):
    anywhere = pl.BlockSpec(memory_space=pl.ANY)
    return pl.pallas_call(
        nothing,
        out_shape=jax.ShapeDtypeStruct(values.shape, values.dtype),
        in_specs=[anywhere] * (1 + len(earlier)),
        out_specs=anywhere,
        input_output_aliases={0: 0},
    )(values, *earlier)


def swap_blocks(values, blocks):
    tok_rows, width = values.shape
    sub = width // blocks
    parts = values.reshape(tok_rows, blocks, sub).transpose(1, 0, 2)
    parts = lax.all_to_all(parts, "tensor", split_axis=0, concat_axis=0, tiled=True)
    return parts.transpose(1, 0, 2).reshape(tok_rows, width)


def exchange(values, bit):
    size = lax.axis_size("dp")
    return lax.ppermute(values, "dp", [(i, i ^ (1 << bit)) for i in range(size)])


def half_of(left, bit, away):
    half = left.shape[1] // 2
    mine = (lax.axis_index("dp") >> bit) & 1
    return lax.dynamic_slice_in_dim(left, (1 - mine if away else mine) * half, half, 1)


def scatter_sum(total, bits):
    me = lax.axis_index("dp")
    for bit in bits[1:]:
        half = total.shape[0] // 2
        mine = (me >> bit) & 1
        away = lax.dynamic_slice_in_dim(total, (1 - mine) * half, half, 0).astype(BF16)
        got = exchange(away, bit)
        total = lax.dynamic_slice_in_dim(total, mine * half, half, 0) + got.astype(F32)
    return total.astype(BF16)


def gather_sum(total, bits):
    me = lax.axis_index("dp")
    for bit in reversed(bits):
        mine = (me >> bit) & 1
        got = exchange(total, bit)
        first = jnp.where(mine == 0, total, got)
        second = jnp.where(mine == 0, got, total)
        total = jnp.concatenate([first, second], axis=0)
    return total


def piece_orders(pieces):
    bits = list(range(lax.axis_size("dp").bit_length() - 1))
    return [bits if piece % 2 == 0 else bits[::-1] for piece in range(pieces)]


def cuts(left, pieces):
    rows = left.shape[1] // pieces
    return [lax.slice_in_dim(left, p * rows, (p + 1) * rows, axis=1) for p in range(pieces)]


def send_products(left, right, pieces):
    orders = piece_orders(pieces)
    away = [
        dot(half_of(cut, order[0], True), right, 0, 0).astype(BF16)
        for cut, order in zip(cuts(left, pieces), orders)
    ]
    return away, [exchange(part, order[0]) for part, order in zip(away, orders)]


def own_shares(left, right, came):
    orders = piece_orders(len(came))
    out = []
    for cut, order, got in zip(cuts(left, len(came)), orders, came):
        kept = dot(half_of(cut, order[0], False), right, 0, 0)
        out.append(scatter_sum(kept + got.astype(F32), order))
    return out


def gathered(shares):
    orders = piece_orders(len(shares))
    return jnp.concatenate([gather_sum(share, order) for share, order in zip(shares, orders)], axis=0)


def on_device(tokens_in, out_grad, left_up, right_up, left_down, right_down):
    blocks = lax.axis_size("tensor")
    first = dot(tokens_in, left_up, 1, 0).astype(BF16)
    mixed_up = swap_blocks(first, blocks)
    back_mixed_down = dot(out_grad, right_down, 1, 1).astype(BF16)
    back_third = swap_blocks(back_mixed_down, blocks)

    pre_act = dot(mixed_up, right_up, 1, 0)
    hidden = gelu_tanh(pre_act).astype(BF16)
    third = dot(hidden, left_down, 1, 0).astype(BF16)
    back_third = after(back_third, third)
    mixed_down = swap_blocks(third, blocks)

    away_left_down, came_left_down = send_products(hidden, back_third, 4)
    back_third = after(back_third, *away_left_down)
    back_hidden = dot(back_third, left_down, 1, 1)
    back_pre = jax.vjp(gelu_tanh, pre_act)[1](back_hidden)[0].astype(BF16)
    back_pre = after(back_pre, mixed_down)
    came_left_down = [after(got, back_pre) for got in came_left_down]
    share_left_down = own_shares(hidden, back_third, came_left_down)
    back_mixed_up = dot(back_pre, right_up, 1, 1).astype(BF16)
    back_first = swap_blocks(back_mixed_up, blocks)
    _, came_right_up = send_products(mixed_up, back_pre, 4)
    came_right_up = [after(got, back_first) for got in came_right_up]
    share_right_up = own_shares(mixed_up, back_pre, came_right_up)
    _, came_right_down = send_products(mixed_down, out_grad, 2)
    share_right_down = own_shares(mixed_down, out_grad, came_right_down)
    _, came_left_up = send_products(tokens_in, back_first, 2)
    share_left_up = own_shares(tokens_in, back_first, came_left_up)
    share_left_down = [after(share, back_first) for share in share_left_down]

    layer_out = dot(mixed_down, right_down, 1, 0).astype(BF16)
    input_grad = dot(back_first, left_up, 1, 1).astype(BF16)
    return (
        layer_out,
        input_grad,
        gathered(share_left_up),
        gathered(share_right_up),
        gathered(share_left_down),
        gathered(share_right_down),
    )


def solution(mesh):
    specs = (P("dp", "tensor"),) * 2 + (P("tensor", None),) * 4
    return jax.shard_map(on_device, mesh=mesh, in_specs=specs, out_specs=specs, check_vma=False)
```
